32 devices in a mesh: section: 4 (over y, core), node: 8 (over z, x).
Axes of the slice: x: 2, y: 2, z: 4, core: 2. Of those that a mesh axis runs over, the one named last changes fastest.
Arguments:
- acts: bfloat16 [4, 3, 2048, 512], P('section', None, 'node'), may hold values from -6 to 6
- top_grad: bfloat16 [3, 2048, 512], P(None, 'node'), may hold values from -6 to 6
- w_in: bfloat16 [4, 512, 1024], P('section'), may hold values from -0.25 to 0.25
- w_out: bfloat16 [4, 1024, 512], P('section'), may hold values from -0.1875 to 0.1875
- tile_table: bfloat16 [3, 64, 128, 128], P(None, 'node'), may hold values from -0.25 to 0.25
- tile_rows: int32 [3, 64], P(None, 'node'), may hold values from 0 to 1
- tile_cols: int32 [3, 64], P(None, 'node'), may hold values from 0 to 15, as said below
- tile_ids: int32 [3, 64], P(None, 'node'), may hold values from 0 to 7
- tile_count: int32 [3, 8], P(None, 'node'), may hold values from 4 to 8, as said below
Outputs:
- act_grads: bfloat16 [4, 3, 2048, 512], P('section', None, 'node')
- w_in_grad: float32 [4, 512, 1024], P('section')
- w_out_grad: float32 [4, 1024, 512], P('section')
The draws below stay inside these ranges and needn't reach their ends.
Inputs may be any that keep to these rules, and one draw needn't show every extreme that they name: `tile_cols`: A tile slot's column block lies on its own device or on the next or previous device along node, wrapping around; of one device's 8 slots at most 2 have columns on the next device and at most 2 on the previous one, and in every group some device has exactly 2 live slots with columns on the next device. Slots k < tile_count of a device are live; in every group some device has 8.
All inputs are finite; a program needn't handle non-finite values.
Results may differ from the reference program's by a relative error of at most 0.03.
Values may be sent and summed in bfloat16 or wider, within the bound.
A program may use at most 64 MiB of HBM per device.

```python
import jax
import jax.numpy as jnp

D = 512
H = 1024
BLK = 128
ROWS = 256
GROUPS = 3
TD = 8
CAP = 2
TABLE = 8
NODES = 2048
LAYERS = 4
N_NODE = 8


def tile_plan(key):
    key = jax.random.fold_in(key, 11)
    devices = NODES // ROWS
    per_device = ROWS // BLK
    keys = jax.random.split(key, 6)
    shape_three = (GROUPS, devices, TD)
    row_pick = jax.random.randint(keys[0], shape_three, 0, per_device)
    direction = jax.random.randint(keys[1], shape_three, 0, 3)
    chosen = jax.random.randint(keys[2], (GROUPS, 1, 1), 0, devices)
    dev_index = jnp.arange(devices, dtype=jnp.int32)[None, :, None]
    slot_index = jnp.arange(TD, dtype=jnp.int32)
    direction = jnp.where((dev_index == chosen) & (slot_index[None, None, :] < CAP), 1, direction)
    earlier = slot_index[None, :] < slot_index[:, None]
    same_dir = direction[..., :, None] == direction[..., None, :]
    ranking = jnp.sum((same_dir & earlier[None, None]).astype(jnp.int32), axis=-1)
    direction = jnp.where((direction > 0) & (ranking >= CAP), 0, direction)
    counts = jax.random.randint(keys[3], (GROUPS, devices), TD // 2, TD + 1)
    counts = jnp.where(jnp.arange(devices)[None, :] == chosen[:, :, 0], TD, counts)
    offset = jnp.where(direction == 1, 1, jnp.where(direction == 2, devices - 1, 0))
    target = (dev_index + offset) % devices
    col_pick = target * per_device + jax.random.randint(keys[4], shape_three, 0, per_device)
    id_pick = jax.random.randint(keys[5], shape_three, 0, TABLE)
    return (row_pick.reshape(GROUPS, devices * TD).astype(jnp.int32), col_pick.reshape(GROUPS, devices * TD).astype(jnp.int32), id_pick.reshape(GROUPS, devices * TD).astype(jnp.int32), counts.astype(jnp.int32))


def draw_tile_rows(key, part):
    return tile_plan(key)[0]


def draw_tile_cols(key, part):
    return tile_plan(key)[1]


def draw_tile_ids(key, part):
    return tile_plan(key)[2]


def draw_tile_count(key, part):
    return tile_plan(key)[3]


def level_of(own_key, extent, shards, low, top_value):
    def one(axis_at, shards_of):
        steps = jax.random.uniform(jax.random.fold_in(jax.random.fold_in(own_key, 6), axis_at), (shards_of,), jnp.float32, low / len(shards), top_value / len(shards))
        return jnp.repeat(jnp.exp(steps), extent[axis_at] // shards_of).reshape((-1,) + (1,) * (len(extent) - axis_at - 1))

    gain = one(*shards[0])
    for cut in shards[1:]:
        gain = gain * one(*cut)
    return gain


def gaussian(own_key, dims, scale, most, shards=(), held_as=jnp.bfloat16):
    result = jax.random.normal(own_key, dims, jnp.float32) * scale
    if len(shards) > 0:
        result = level_of(own_key, dims, shards, -0.22, 0.18) * result
    return jnp.clip(result, min=-most, max=most).astype(held_as)


def setup_inputs(seed: int = 0) -> dict:
    seeds = jax.random.split(jax.random.key(seed), 10)
    acts = gaussian(seeds[0], (LAYERS, GROUPS, NODES, D), 1.0, 6.0, ((0, 4), (2, 8)))
    top_grad = gaussian(seeds[1], (GROUPS, NODES, D), 1.0, 6.0, ((1, 8),))
    w_in = gaussian(seeds[2], (LAYERS, D, H), D ** -0.5, 0.25, ((0, 4),))
    w_out = gaussian(seeds[3], (LAYERS, H, D), H ** -0.5, 0.1875, ((0, 4),))
    tile_table = gaussian(seeds[4], (GROUPS, TABLE * N_NODE, BLK, BLK), (4 * BLK) ** -0.5, 0.25, ((1, 8),))
    tile_rows = draw_tile_rows(jax.random.fold_in(seeds[9], 71), 0)
    tile_cols = draw_tile_cols(jax.random.fold_in(seeds[9], 71), 0)
    tile_ids = draw_tile_ids(jax.random.fold_in(seeds[9], 71), 0)
    tile_count = draw_tile_count(jax.random.fold_in(seeds[9], 71), 0)
    return {"acts": acts, "top_grad": top_grad, "w_in": w_in, "w_out": w_out, "tile_table": tile_table, "tile_rows": tile_rows, "tile_cols": tile_cols, "tile_ids": tile_ids, "tile_count": tile_count}


def reference(acts, top_grad, w_in, w_out, tile_table, tile_rows, tile_cols, tile_ids, tile_count):
    block_count = NODES // BLK
    devices = NODES // ROWS
    per_device = ROWS // BLK
    slot_dev = jnp.arange(devices * TD, dtype=jnp.int32) // TD
    slot_pos = jnp.arange(devices * TD, dtype=jnp.int32) % TD
    grads_all = []
    first_sum = [jnp.zeros((D, H), jnp.float32) for layer_idx in range(LAYERS)]
    second_sum = [jnp.zeros((H, D), jnp.float32) for layer_idx in range(LAYERS)]
    for group_idx in range(GROUPS):
        live_mask = slot_pos < tile_count[group_idx][slot_dev]
        row_glob = (slot_dev * per_device + tile_rows[group_idx]).astype(jnp.int32)
        table_idx = (slot_dev * TABLE + tile_ids[group_idx]).astype(jnp.int32)
        tile_vals = tile_table[group_idx][table_idx].astype(jnp.float32)
        grad_now = top_grad[group_idx]
        per_layer = [None] * LAYERS
        for layer_idx in range(LAYERS - 1, -1, -1):
            pieces = grad_now.reshape(block_count, BLK, D)[row_glob].astype(jnp.float32)
            terms = jnp.einsum('kij,kid->kjd', tile_vals, pieces).astype(jnp.bfloat16)
            terms = jnp.where(live_mask[:, None, None], terms.astype(jnp.float32), 0.0)
            summed = jax.ops.segment_sum(terms, tile_cols[group_idx], num_segments=block_count)
            grad_mid = summed.reshape(NODES, D).astype(jnp.bfloat16)
            layer_in = acts[layer_idx, group_idx]
            pre = jnp.dot(layer_in, w_in[layer_idx], preferred_element_type=jnp.float32)
            sigma = jax.nn.sigmoid(pre)
            act_val = (pre * sigma).astype(jnp.bfloat16)
            second_sum[layer_idx] = second_sum[layer_idx] + jnp.dot(act_val.T, grad_mid, preferred_element_type=jnp.float32)
            dact = jnp.dot(grad_mid, w_out[layer_idx].T, preferred_element_type=jnp.float32)
            dpre = (dact * sigma * (1.0 + pre * (1.0 - sigma))).astype(jnp.bfloat16)
            first_sum[layer_idx] = first_sum[layer_idx] + jnp.dot(layer_in.T, dpre, preferred_element_type=jnp.float32)
            back = jnp.dot(dpre, w_in[layer_idx].T, preferred_element_type=jnp.float32)
            grad_now = (grad_now.astype(jnp.float32) + back).astype(jnp.bfloat16)
            per_layer[layer_idx] = grad_now
        grads_all.append(jnp.stack(per_layer))
    act_grads = jnp.stack(grads_all, axis=1)
    return act_grads, jnp.stack(first_sum), jnp.stack(second_sum)
```

```python
import functools

import jax
import jax.numpy as jnp
from jax import lax
from jax.experimental import pallas as pl
from jax.experimental.pallas import tpu as pltpu
from jax.sharding import PartitionSpec as P

MESH = pl.DeviceIdType.MESH
F32 = jnp.float32
BF16 = jnp.bfloat16
CHUNKS = 4
CONTRACT_LAST = (((1,), (1,)), ((), ()))
CONTRACT_FIRST = (((0,), (0,)), ((), ()))


def dot(a, b, dims=(((1,), (0,)), ((), ()))):
    return lax.dot_general(a, b, dims, preferred_element_type=F32)


def kernel(
    sections, nodes,
    rows_ref, cols_ref, ids_ref, count_ref, acts_ref, top_ref, w1_ref, w2_ref, table_ref,
    grads_ref, first_ref, second_ref,
    adj, g_in, to_next, to_prev, from_prev, from_next, act_s, slope_s, dm_s, dpre_s, acc1, acc2,
    send_x1, send_x2, recv_x1, recv_x2, send_z1, send_z2, recv_z1, recv_z2,
    term_ssem, term_rsem, hand_ssem, hand_rsem, x_ssem, x_rsem, z_ssem, z_rsem, az_ssem, az_rsem, ax_ssem, ax_rsem,
):
    groups, rows, feat = top_ref.shape
    hidden = w1_ref.shape[2]
    slots = rows_ref.shape[1]
    blk = table_ref.shape[-1]
    blocks = rows // blk
    sec = lax.axis_index("section")
    node = lax.axis_index("node")
    nxt = lax.rem(node + 1, nodes)
    prv = lax.rem(node + nodes - 1, nodes)
    line = nodes // 2
    along = node // 2
    side = lax.rem(node, 2)
    partner = node + 1 - 2 * side
    top_sec = sec == sections - 1
    has_below = sec > 0
    has_up = along < line - 1
    has_down = along > 0

    def remote(src, dst, ssem, rsem, node_to, sec_to=None):
        return pltpu.make_async_remote_copy(
            src_ref=src, dst_ref=dst, send_sem=ssem, recv_sem=rsem,
            device_id=(sec if sec_to is None else sec_to, node_to), device_id_type=MESH,
        )

    barrier = pltpu.get_barrier_semaphore()

    def greet(section_to, node_to):
        pl.semaphore_signal(barrier, inc=1, device_id=(section_to, node_to), device_id_type=MESH)

    greet(sec, nxt)
    greet(sec, prv)
    greet(sec, partner)
    pl.when(has_below)(lambda: greet(sec - 1, node))
    pl.when(jnp.logical_not(top_sec))(lambda: greet(sec + 1, node))
    pl.when(has_up)(lambda: greet(sec, node + 2))
    pl.when(has_down)(lambda: greet(sec, node - 2))

    def build(c):
        for d, owner in enumerate((node, nxt, prv)):
            for cb in range(blocks):
                col = owner * blocks + cb
                for r in range(blocks):
                    total = jnp.zeros((blk, blk), F32)
                    for k in range(slots):
                        live = (k < count_ref[c, 0]) & (rows_ref[c, k] == r) & (cols_ref[c, k] == col)
                        coef = jnp.where(live, 1.0, 0.0).astype(F32)
                        total = total + coef * table_ref[c, ids_ref[c, k]].astype(F32)
                    place = (d * blocks + cb) * blk
                    adj[c, place:place + blk, r * blk:(r + 1) * blk] = total.T.astype(BF16)

    def forward(c):
        h = acts_ref[0, c]
        step = hidden // 4
        for j in range(4):
            at = slice(j * step, (j + 1) * step)
            pre = dot(h, w1_ref[0, :, at])
            sigma = jax.nn.sigmoid(pre)
            act_s[c, :, at] = (pre * sigma).astype(BF16)
            slope_s[c, :, at] = sigma * (1.0 + pre * (1.0 - sigma))

    def weight_grads(c):
        def put(ref, at, value):
            if c == 0:
                ref[at, :] = value
            else:
                ref[at, :] += value

        step = hidden // 4
        for j in range(4):
            at = slice(j * step, (j + 1) * step)
            put(acc2, at, dot(act_s[c, :, at], dm_s[c], CONTRACT_FIRST))
        step = feat // 4
        for j in range(4):
            at = slice(j * step, (j + 1) * step)
            put(acc1, at, dot(acts_ref[0, c, :, at], dpre_s[c], CONTRACT_FIRST))

    def hand(c):
        return remote(grads_ref.at[0, c], g_in.at[c], hand_ssem.at[c], hand_rsem.at[c], node, sec - 1)

    build(0)
    greeted = 3 + has_below.astype(jnp.int32) + jnp.logical_not(top_sec).astype(jnp.int32)
    greeted = greeted + has_up.astype(jnp.int32) + has_down.astype(jnp.int32)
    pl.semaphore_wait(barrier, greeted)

    for c in range(groups):
        @pl.when(top_sec)
        def _():
            g_in[c] = top_ref[c]

        @pl.when(jnp.logical_not(top_sec))
        def _():
            hand(c).wait_recv()

        grad = g_in[c]
        to_next[c] = dot(adj[c, rows:2 * rows], grad).astype(BF16)
        ahead = remote(to_next.at[c], from_prev.at[c], term_ssem.at[c, 0], term_rsem.at[c, 0], nxt)
        ahead.start()
        to_prev[c] = dot(adj[c, 2 * rows:], grad).astype(BF16)
        back = remote(to_prev.at[c], from_next.at[c], term_ssem.at[c, 1], term_rsem.at[c, 1], prv)
        back.start()
        local = dot(adj[c, :rows], grad)
        forward(c)
        if c + 1 < groups:
            build(c + 1)
        if c > 0:
            weight_grads(c - 1)
        ahead.wait_recv()
        back.wait_recv()
        mid = (local + from_prev[c].astype(F32) + from_next[c].astype(F32)).astype(BF16)
        dm_s[c] = mid
        step = hidden // 4
        for j in range(4):
            at = slice(j * step, (j + 1) * step)
            dact = dot(mid, w2_ref[0, at, :], CONTRACT_LAST)
            dpre_s[c, :, at] = (dact * slope_s[c, :, at]).astype(BF16)
        new_grad = g_in[c].astype(F32) + dot(dpre_s[c], w1_ref[0], CONTRACT_LAST)
        grads_ref[0, c] = new_grad.astype(BF16)
        pl.when(has_below)(lambda: hand(c).start())

    weight_grads(groups - 1)
    half1 = feat // 2
    half2 = hidden // 2
    step1 = half1 // CHUNKS
    step2 = half2 // CHUNKS

    def own(kind, j):
        if kind == 0:
            return pl.ds(pl.multiple_of(side * half1 + j * step1, step1), step1)
        return pl.ds(pl.multiple_of(side * half2 + j * step2, step2), step2)

    def other(kind, j):
        if kind == 0:
            return pl.ds(pl.multiple_of((1 - side) * half1 + j * step1, step1), step1)
        return pl.ds(pl.multiple_of((1 - side) * half2 + j * step2, step2), step2)

    acc = (acc1, acc2)
    outs = (first_ref, second_ref)
    send_x, recv_x = (send_x1, send_x2), (recv_x1, recv_x2)
    send_z, recv_z = (send_z1, send_z2), (recv_z1, recv_z2)
    towards = (node + 2, node - 2)
    away = (node - 2, node + 2)
    has_towards = (has_up, has_down)
    has_away = (has_down, has_up)

    def x_copy(kind, j):
        return remote(
            send_x[kind].at[j], recv_x[kind].at[j], x_ssem.at[kind, j], x_rsem.at[kind, j], partner)

    def z_copy(kind, j):
        return remote(
            send_z[kind].at[j], recv_z[kind].at[j], z_ssem.at[kind, j], z_rsem.at[kind, j], towards[kind])

    def az_copy(kind, j):
        place = outs[kind].at[own(kind, j), :]
        return remote(place, place, az_ssem.at[kind, j], az_rsem.at[kind, j], away[kind])

    def ax_copy(kind, j):
        place = outs[kind].at[own(kind, j), :]
        return remote(place, place, ax_ssem.at[kind, j], ax_rsem.at[kind, j], partner)

    for j in range(CHUNKS):
        for kind in range(2):
            send_x[kind][j] = acc[kind][other(kind, j), :].astype(BF16)
            x_copy(kind, j).start()

    def reduce_chunk(kind, j):
        x_copy(kind, j).wait_recv()
        value = acc[kind][own(kind, j), :] + recv_x[kind][j].astype(F32)
        send_z[kind][j] = value.astype(BF16)

        @pl.when(has_away[kind])
        def _():
            z_copy(kind, j).wait_recv()
            send_z[kind][j] = (value + recv_z[kind][j].astype(F32)).astype(BF16)

        @pl.when(has_towards[kind])
        def _():
            z_copy(kind, j).start()

        @pl.when(jnp.logical_not(has_towards[kind]))
        def _():
            outs[kind][own(kind, j), :] = send_z[kind][j]
            az_copy(kind, j).start()
            ax_copy(kind, j).start()

    def gather_chunk(kind, j):
        @pl.when(has_towards[kind])
        def _():
            az_copy(kind, j).wait_recv()
            pl.when(has_away[kind])(lambda: az_copy(kind, j).start())
            ax_copy(kind, j).start()

    def in_order(step):
        def run(first):
            for kind in (first, 1 - first):
                for j in range(CHUNKS):
                    step(kind, j)

        return run

    early = along < line // 2
    late = jnp.logical_not(early)
    pl.when(early)(lambda: in_order(reduce_chunk)(0))
    pl.when(late)(lambda: in_order(reduce_chunk)(1))
    pl.when(early)(lambda: in_order(gather_chunk)(1))
    pl.when(late)(lambda: in_order(gather_chunk)(0))

    for kind in range(2):
        for j in range(CHUNKS):
            ax_copy(kind, j).wait()
            x_copy(kind, j).wait_send()
            pl.when(has_towards[kind])(lambda: z_copy(kind, j).wait_send())
            pl.when(has_away[kind])(lambda: az_copy(kind, j).wait_send())
    for c in range(groups):
        remote(to_next.at[c], from_prev.at[c], term_ssem.at[c, 0], term_rsem.at[c, 0], nxt).wait_send()
        remote(to_prev.at[c], from_next.at[c], term_ssem.at[c, 1], term_rsem.at[c, 1], prv).wait_send()
        pl.when(has_below)(lambda: hand(c).wait_send())


def shards(acts, top_grad, w_in, w_out, tile_table, tile_rows, tile_cols, tile_ids, tile_count):
    sections = lax.axis_size("section")
    nodes = lax.axis_size("node")
    groups, rows, feat = top_grad.shape
    hidden = w_in.shape[2]
    vmem = pl.BlockSpec(memory_space=pltpu.VMEM)
    smem = pl.BlockSpec(memory_space=pltpu.SMEM)
    wide = lambda kind, count: pltpu.VMEM((groups, rows, count), kind)
    part1 = pltpu.VMEM((CHUNKS, feat // 2 // CHUNKS, hidden), BF16)
    part2 = pltpu.VMEM((CHUNKS, hidden // 2 // CHUNKS, feat), BF16)
    dma = pltpu.SemaphoreType.DMA
    grads, first, second = pl.pallas_call(
        functools.partial(kernel, sections, nodes),
        out_shape=(
            jax.ShapeDtypeStruct((1, groups, rows, feat), BF16),
            jax.ShapeDtypeStruct((feat, hidden), BF16),
            jax.ShapeDtypeStruct((hidden, feat), BF16),
        ),
        in_specs=[smem] * 4 + [vmem] * 5,
        out_specs=(vmem, vmem, vmem),
        scratch_shapes=[
            pltpu.VMEM((groups, 3 * rows, rows), BF16),
            *[wide(BF16, feat)] * 5,
            wide(BF16, hidden),
            wide(F32, hidden),
            wide(BF16, feat),
            wide(BF16, hidden),
            pltpu.VMEM((feat, hidden), F32),
            pltpu.VMEM((hidden, feat), F32),
            *[part1, part2] * 4,
            dma((groups, 2)), dma((groups, 2)), dma((groups,)), dma((groups,)),
            *[dma((2, CHUNKS))] * 8,
        ],
        compiler_params=pltpu.CompilerParams(
            collective_id=0, has_side_effects=True, vmem_limit_bytes=48 * 1024 * 1024
        ),
        name="relay_back",
    )(tile_rows, tile_cols, tile_ids, tile_count, acts, top_grad, w_in, w_out, tile_table)
    return grads, first.astype(F32)[None], second.astype(F32)[None]


def solution(mesh):
    return jax.shard_map(
        shards,
        mesh=mesh,
        in_specs=(
            P("section", None, "node", None),
            P(None, "node", None),
            P("section", None, None),
            P("section", None, None),
            P(None, "node", None, None),
            P(None, "node"),
            P(None, "node"),
            P(None, "node"),
            P(None, "node"),
        ),
        out_specs=(
            P("section", None, "node", None),
            P("section", None, None),
            P("section", None, None),
        ),
        check_vma=False,
    )
```

```python
import functools

import jax
import jax.numpy as jnp
from jax import lax
from jax.experimental import pallas as pl
from jax.experimental.pallas import tpu as pltpu
from jax.sharding import PartitionSpec as P

MESH = pl.DeviceIdType.MESH
F32 = jnp.float32
BF16 = jnp.bfloat16
CHUNKS = 4
HALVES = 2
CONTRACT_LAST = (((1,), (1,)), ((), ()))
CONTRACT_FIRST = (((0,), (0,)), ((), ()))


def dot(a, b, dims=(((1,), (0,)), ((), ()))):
    return lax.dot_general(a, b, dims, preferred_element_type=F32)


def kernel(
    sections, nodes,
    rows_ref, cols_ref, ids_ref, count_ref, acts_hbm, top_hbm, w1_hbm, w2_hbm, table_hbm,
    grads_ref, first_ref, second_ref,
    acts_ref, top_ref, w1_ref, w2_ref, table_ref, load_sem,
    adj_own, adj_out, adj_par, g_own, g_par, g_out, to_line, from_line, act_s, slope_s, dm_s, dpre_s, acc1, acc2,
    send_x1, send_x2, recv_x1, recv_x2, send_z1, send_z2, recv_z1, recv_z2,
    adj_ssem, adj_rsem, pass_ssem, own_ssem, own_rsem, par_ssem, par_rsem, term_ssem, term_rsem,
    x_ssem, x_rsem, z_ssem, z_rsem, az_ssem, az_rsem, ax_ssem, ax_rsem,
):
    groups, halves, rows, width = g_own.shape
    feat = halves * width
    hidden = w1_ref.shape[2]
    slots = rows_ref.shape[1]
    blk = table_ref.shape[-1]
    blocks = rows // blk
    sec = lax.axis_index("section")
    node = lax.axis_index("node")
    line = nodes // 2
    along = node // 2
    side = lax.rem(node, 2)
    partner = node + 1 - 2 * side
    outer = lax.rem(node + nodes - 1 + 2 * side, nodes)
    line_to = lax.rem(node + 2 + side * (nodes - 4), nodes)
    line_from = lax.rem(node + nodes - 2 + side * (4 - nodes) + side * nodes, nodes)
    top_sec = sec == sections - 1
    below_top = sec < sections - 1
    has_below = sec > 0
    odd = lax.rem(sec, 2) == 1
    even = lax.rem(sec, 2) == 0
    has_up = along < line - 1
    has_down = along > 0

    def remote(src, dst, ssem, rsem, node_to, sec_to=None):
        return pltpu.make_async_remote_copy(
            src_ref=src, dst_ref=dst, send_sem=ssem, recv_sem=rsem,
            device_id=(sec if sec_to is None else sec_to, node_to), device_id_type=MESH,
        )

    barrier = pltpu.get_barrier_semaphore()

    def greet(section_to, node_to):
        pl.semaphore_signal(barrier, inc=1, device_id=(section_to, node_to), device_id_type=MESH)

    greet(sec, partner)
    greet(sec, line_to)
    greet(sec, line_from)
    pl.when(odd)(lambda: greet(sec - 1, partner))
    pl.when(even)(lambda: greet(sec + 1, partner))
    pl.when(has_below)(lambda: greet(sec - 1, node))
    pl.when(below_top)(lambda: greet(sec + 1, node))

    def load(at, src, dst):
        return pltpu.make_async_copy(src, dst, load_sem.at[at])

    load_table = load(0, table_hbm, table_ref)
    load_acts = load(1, acts_hbm, acts_ref)
    load_w1 = load(2, w1_hbm, w1_ref)
    load_w2 = load(3, w2_hbm, w2_ref)
    load_table.start()
    pl.when(top_sec)(lambda: load(4, top_hbm, top_ref).start())
    load_acts.start()
    load_w1.start()
    load_w2.start()

    def block(c, owner, cb, r):
        total = jnp.zeros((blk, blk), F32)
        for k in range(slots):
            live = (k < count_ref[c, 0]) & (rows_ref[c, k] == r) & (cols_ref[c, k] == owner * blocks + cb)
            coef = jnp.where(live, 1.0, 0.0).astype(F32)
            total = total + coef * table_ref[c, ids_ref[c, k]].astype(F32)
        return total.T.astype(BF16)

    def adj_copy(c):
        return remote(adj_out.at[c], adj_par.at[c], adj_ssem.at[c], adj_rsem.at[c], partner)

    def pass_copy(c):
        return remote(adj_par.at[c], adj_par.at[c], pass_ssem.at[c], adj_rsem.at[c], node, sec - 1)

    def own_copy(c, f):
        return remote(
            g_out.at[c, f], g_own.at[c, f], own_ssem.at[c, f], own_rsem.at[c, f], node, sec - 1)

    def par_copy(c, f):
        return remote(
            g_out.at[c, f], g_par.at[c, f], par_ssem.at[c, f], par_rsem.at[c, f], partner, sec - 1)

    def relay_copy(c, f):
        return remote(
            g_own.at[c, f], g_par.at[c, f], par_ssem.at[groups + c, f], par_rsem.at[c, f], partner)

    def line_copy(c, f):
        return remote(
            to_line.at[c, f], from_line.at[c, f], term_ssem.at[c, f], term_rsem.at[c, f], line_to)

    def build(c):
        @pl.when(odd)
        def _():
            for d, owner in enumerate((partner, outer)):
                for cb in range(blocks):
                    for r in range(blocks):
                        place = (d * blocks + cb) * blk
                        adj_out[c, place:place + blk, r * blk:(r + 1) * blk] = block(c, owner, cb, r)
            adj_copy(c).start()

        for cb in range(blocks):
            for r in range(blocks):
                adj_own[c, cb * blk:(cb + 1) * blk, r * blk:(r + 1) * blk] = block(c, node, cb, r)

    def take_top(c):
        for f in range(halves):
            g_own[c, f] = top_ref[c, :, f * width:(f + 1) * width]
            relay_copy(c, f).start()

    def forward(c):
        step = hidden // 4
        for j in range(4):
            at = slice(j * step, (j + 1) * step)
            pre = dot(acts_ref[0, c], w1_ref[0, :, at])
            sigma = jax.nn.sigmoid(pre)
            act_s[c, :, at] = (pre * sigma).astype(BF16)
            slope_s[c, :, at] = sigma * (1.0 + pre * (1.0 - sigma))

    def weight_grads(c):
        def put(ref, at, value):
            if c == 0:
                ref[at, :] = value
            else:
                ref[at, :] += value

        step = hidden // 4
        for j in range(4):
            at = slice(j * step, (j + 1) * step)
            put(acc2, at, dot(act_s[c, :, at], dm_s[c], CONTRACT_FIRST))
        step = feat // 4
        for j in range(4):
            at = slice(j * step, (j + 1) * step)
            put(acc1, at, dot(acts_ref[0, c, :, at], dpre_s[c], CONTRACT_FIRST))

    greeted = 4 + has_below.astype(jnp.int32) + below_top.astype(jnp.int32)
    pl.semaphore_wait(barrier, greeted)

    @pl.when(top_sec)
    def _():
        load(4, top_hbm, top_ref).wait()
        take_top(0)

    load_table.wait()
    build(0)
    load_acts.wait()
    load_w1.wait()
    load_w2.wait()

    @pl.when(below_top)
    def _():
        for c in range(1, groups):
            build(c)
        for c in range(groups):
            forward(c)

    for c in range(groups):
        @pl.when(below_top)
        def _():
            for f in range(halves):
                own_copy(c, f).wait_recv()
                pl.when(odd)(lambda: relay_copy(c, f).start())

        local = [dot(adj_own[c], g_own[c, f]) for f in range(halves)]
        adj_copy(c).wait_recv()
        pl.when(odd)(lambda: pass_copy(c).start())
        for f in range(halves):
            par_copy(c, f).wait_recv()
            to_line[c, f] = dot(adj_par[c, rows:], g_par[c, f]).astype(BF16)
            line_copy(c, f).start()
            local[f] = local[f] + dot(adj_par[c, :rows], g_par[c, f])

        @pl.when(top_sec)
        def _():
            if c + 1 < groups:
                take_top(c + 1)
                build(c + 1)
            forward(c)

        if c > 0:
            weight_grads(c - 1)
        for f in range(halves):
            line_copy(c, f).wait_recv()
            dm_s[c, :, f * width:(f + 1) * width] = (local[f] + from_line[c, f].astype(F32)).astype(BF16)
        step = hidden // 4
        for j in range(4):
            at = slice(j * step, (j + 1) * step)
            dact = dot(dm_s[c], w2_ref[0, at, :], CONTRACT_LAST)
            dpre_s[c, :, at] = (dact * slope_s[c, :, at]).astype(BF16)
        for f in range(halves):
            at = slice(f * width, (f + 1) * width)
            back = dot(dpre_s[c], w1_ref[0, at, :], CONTRACT_LAST)
            g_out[c, f] = (g_own[c, f].astype(F32) + back).astype(BF16)
            pl.when(has_below)(lambda: own_copy(c, f).start())
            pl.when(odd)(lambda: par_copy(c, f).start())
            grads_ref[0, c, :, at] = g_out[c, f]

    weight_grads(groups - 1)
    half1 = feat // 2
    half2 = hidden // 2
    step1 = half1 // CHUNKS
    step2 = half2 // CHUNKS

    def own(kind, j):
        if kind == 0:
            return pl.ds(pl.multiple_of(side * half1 + j * step1, step1), step1)
        return pl.ds(pl.multiple_of(side * half2 + j * step2, step2), step2)

    def other(kind, j):
        if kind == 0:
            return pl.ds(pl.multiple_of((1 - side) * half1 + j * step1, step1), step1)
        return pl.ds(pl.multiple_of((1 - side) * half2 + j * step2, step2), step2)

    acc = (acc1, acc2)
    outs = (first_ref, second_ref)
    send_x, recv_x = (send_x1, send_x2), (recv_x1, recv_x2)
    send_z, recv_z = (send_z1, send_z2), (recv_z1, recv_z2)
    towards = (node + 2, node - 2)
    away = (node - 2, node + 2)
    has_towards = (has_up, has_down)
    has_away = (has_down, has_up)

    def x_copy(kind, j):
        return remote(
            send_x[kind].at[j], recv_x[kind].at[j], x_ssem.at[kind, j], x_rsem.at[kind, j], partner)

    def z_copy(kind, j):
        return remote(
            send_z[kind].at[j], recv_z[kind].at[j], z_ssem.at[kind, j], z_rsem.at[kind, j], towards[kind])

    def az_copy(kind, j):
        place = outs[kind].at[own(kind, j), :]
        return remote(place, place, az_ssem.at[kind, j], az_rsem.at[kind, j], away[kind])

    def ax_copy(kind, j):
        place = outs[kind].at[own(kind, j), :]
        return remote(place, place, ax_ssem.at[kind, j], ax_rsem.at[kind, j], partner)

    for j in range(CHUNKS):
        for kind in range(2):
            send_x[kind][j] = acc[kind][other(kind, j), :].astype(BF16)
            x_copy(kind, j).start()

    def reduce_chunk(kind, j):
        x_copy(kind, j).wait_recv()
        value = acc[kind][own(kind, j), :] + recv_x[kind][j].astype(F32)
        send_z[kind][j] = value.astype(BF16)

        @pl.when(has_away[kind])
        def _():
            z_copy(kind, j).wait_recv()
            send_z[kind][j] = (value + recv_z[kind][j].astype(F32)).astype(BF16)

        @pl.when(has_towards[kind])
        def _():
            z_copy(kind, j).start()

        @pl.when(jnp.logical_not(has_towards[kind]))
        def _():
            outs[kind][own(kind, j), :] = send_z[kind][j]
            az_copy(kind, j).start()
            ax_copy(kind, j).start()

    def gather_chunk(kind, j):
        @pl.when(has_towards[kind])
        def _():
            az_copy(kind, j).wait_recv()
            pl.when(has_away[kind])(lambda: az_copy(kind, j).start())
            ax_copy(kind, j).start()

    def in_order(step):
        def run(first):
            for kind in (first, 1 - first):
                for j in range(CHUNKS):
                    step(kind, j)

        return run

    early = along < line // 2
    late = jnp.logical_not(early)
    pl.when(early)(lambda: in_order(reduce_chunk)(0))
    pl.when(late)(lambda: in_order(reduce_chunk)(1))
    pl.when(early)(lambda: in_order(gather_chunk)(1))
    pl.when(late)(lambda: in_order(gather_chunk)(0))

    for kind in range(2):
        for j in range(CHUNKS):
            ax_copy(kind, j).wait()
            x_copy(kind, j).wait_send()
            pl.when(has_towards[kind])(lambda: z_copy(kind, j).wait_send())
            pl.when(has_away[kind])(lambda: az_copy(kind, j).wait_send())
    for c in range(groups):
        @pl.when(odd)
        def _():
            adj_copy(c).wait_send()
            pass_copy(c).wait_send()

        for f in range(halves):
            line_copy(c, f).wait_send()
            pl.when(has_below)(lambda: own_copy(c, f).wait_send())

            @pl.when(odd)
            def _():
                par_copy(c, f).wait_send()
                relay_copy(c, f).wait_send()


def shards(acts, top_grad, w_in, w_out, tile_table, tile_rows, tile_cols, tile_ids, tile_count):
    sections = lax.axis_size("section")
    nodes = lax.axis_size("node")
    groups, rows, feat = top_grad.shape
    hidden = w_in.shape[2]
    vmem = pl.BlockSpec(memory_space=pltpu.VMEM)
    hbm = pl.BlockSpec(memory_space=pltpu.HBM)
    smem = pl.BlockSpec(memory_space=pltpu.SMEM)
    width = feat // HALVES
    half = pltpu.VMEM((groups, HALVES, rows, width), BF16)
    wide = lambda kind, count: pltpu.VMEM((groups, rows, count), kind)
    part1 = pltpu.VMEM((CHUNKS, feat // 2 // CHUNKS, hidden), BF16)
    part2 = pltpu.VMEM((CHUNKS, hidden // 2 // CHUNKS, feat), BF16)
    dma = pltpu.SemaphoreType.DMA
    grads, first, second = pl.pallas_call(
        functools.partial(kernel, sections, nodes),
        out_shape=(
            jax.ShapeDtypeStruct((1, groups, rows, feat), BF16),
            jax.ShapeDtypeStruct((feat, hidden), BF16),
            jax.ShapeDtypeStruct((hidden, feat), BF16),
        ),
        in_specs=[smem] * 4 + [hbm] * 5,
        out_specs=(vmem, vmem, vmem),
        scratch_shapes=[
            *[pltpu.VMEM(arg.shape, BF16) for arg in (acts, top_grad, w_in, w_out, tile_table)],
            dma((5,)),
            pltpu.VMEM((groups, rows, rows), BF16),
            *[pltpu.VMEM((groups, 2 * rows, rows), BF16)] * 2,
            *[half] * 5,
            wide(BF16, hidden),
            wide(F32, hidden),
            wide(BF16, feat),
            wide(BF16, hidden),
            pltpu.VMEM((feat, hidden), F32),
            pltpu.VMEM((hidden, feat), F32),
            *[part1, part2] * 4,
            *[dma((groups,))] * 3,
            *[dma((groups, HALVES))] * 2,
            dma((2 * groups, HALVES)),
            *[dma((groups, HALVES))] * 3,
            *[dma((2, CHUNKS))] * 8,
        ],
        compiler_params=pltpu.CompilerParams(
            collective_id=0, has_side_effects=True, vmem_limit_bytes=48 * 1024 * 1024
        ),
        name="relay_back",
    )(tile_rows, tile_cols, tile_ids, tile_count, acts, top_grad, w_in, w_out, tile_table)
    return grads, first.astype(F32)[None], second.astype(F32)[None]


def solution(mesh):
    return jax.shard_map(
        shards,
        mesh=mesh,
        in_specs=(
            P("section", None, "node", None),
            P(None, "node", None),
            P("section", None, None),
            P("section", None, None),
            P(None, "node", None, None),
            P(None, "node"),
            P(None, "node"),
            P(None, "node"),
            P(None, "node"),
        ),
        out_specs=(
            P("section", None, "node", None),
            P("section", None, None),
            P("section", None, None),
        ),
        check_vma=False,
    )
```

```python
import functools

import jax
import jax.numpy as jnp
from jax import lax
from jax.experimental import pallas as pl
from jax.experimental.pallas import tpu as pltpu
from jax.sharding import PartitionSpec as P

MESH = pl.DeviceIdType.MESH
F32 = jnp.float32
BF16 = jnp.bfloat16
CHUNKS = 8
AHEAD = 3
HALVES = 2
CONTRACT_LAST = (((1,), (1,)), ((), ()))
CONTRACT_FIRST = (((0,), (0,)), ((), ()))


def dot(a, b, dims=(((1,), (0,)), ((), ()))):
    return lax.dot_general(a, b, dims, preferred_element_type=F32)


def kernel(
    sections, nodes,
    rows_ref, cols_ref, ids_ref, count_ref, acts_hbm, top_hbm, w1_hbm, w2_hbm, table_hbm,
    grads_ref, first_ref, second_ref,
    acts_ref, top_ref, w1_ref, w2_ref, table_ref, load_sem,
    adj_own, adj_out, adj_par, g_own, g_par, g_out, to_line, from_line, act_s, slope_s, dm_s, dpre_s, acc1, acc2,
    send_x1, send_x2, recv_x1, recv_x2, send_z1, send_z2, recv_z1, recv_z2,
    adj_ssem, adj_rsem, pass_ssem, own_ssem, own_rsem, par_ssem, par_rsem, term_ssem, term_rsem,
    x_ssem, x_rsem, z_ssem, z_rsem, az_ssem, az_rsem, ax_ssem, ax_rsem,
):
    groups, halves, rows, width = g_own.shape
    feat = halves * width
    hidden = w1_ref.shape[2]
    slots = rows_ref.shape[1]
    blk = table_ref.shape[-1]
    blocks = rows // blk
    sec = lax.axis_index("section")
    node = lax.axis_index("node")
    line = nodes // 2
    along = node // 2
    side = lax.rem(node, 2)
    partner = node + 1 - 2 * side
    outer = lax.rem(node + nodes - 1 + 2 * side, nodes)
    line_to = lax.rem(node + 2 + side * (nodes - 4), nodes)
    line_from = lax.rem(node + nodes - 2 + side * (4 - nodes) + side * nodes, nodes)
    top_sec = sec == sections - 1
    below_top = sec < sections - 1
    has_below = sec > 0
    odd = lax.rem(sec, 2) == 1
    even = lax.rem(sec, 2) == 0
    has_up = along < line - 1
    has_down = along > 0

    def remote(src, dst, ssem, rsem, node_to, sec_to=None):
        return pltpu.make_async_remote_copy(
            src_ref=src, dst_ref=dst, send_sem=ssem, recv_sem=rsem,
            device_id=(sec if sec_to is None else sec_to, node_to), device_id_type=MESH,
        )

    barrier = pltpu.get_barrier_semaphore()

    def greet(section_to, node_to):
        pl.semaphore_signal(barrier, inc=1, device_id=(section_to, node_to), device_id_type=MESH)

    greet(sec, partner)
    greet(sec, line_to)
    greet(sec, line_from)
    pl.when(odd)(lambda: greet(sec - 1, partner))
    pl.when(even)(lambda: greet(sec + 1, partner))
    pl.when(has_below)(lambda: greet(sec - 1, node))
    pl.when(below_top)(lambda: greet(sec + 1, node))

    def load(at, src, dst):
        return pltpu.make_async_copy(src, dst, load_sem.at[at])

    load_table = load(0, table_hbm, table_ref)
    load_acts = load(1, acts_hbm, acts_ref)
    load_w1 = load(2, w1_hbm, w1_ref)
    load_w2 = load(3, w2_hbm, w2_ref)
    load_table.start()
    pl.when(top_sec)(lambda: load(4, top_hbm, top_ref).start())
    load_acts.start()
    load_w1.start()
    load_w2.start()

    def block(c, owner, cb, r):
        total = jnp.zeros((blk, blk), F32)
        for k in range(slots):
            live = (k < count_ref[c, 0]) & (rows_ref[c, k] == r) & (cols_ref[c, k] == owner * blocks + cb)
            coef = jnp.where(live, 1.0, 0.0).astype(F32)
            total = total + coef * table_ref[c, ids_ref[c, k]].astype(F32)
        return total.T.astype(BF16)

    def adj_copy(c):
        return remote(adj_out.at[c], adj_par.at[c], adj_ssem.at[c], adj_rsem.at[c], partner)

    def pass_copy(c):
        return remote(adj_par.at[c], adj_par.at[c], pass_ssem.at[c], adj_rsem.at[c], node, sec - 1)

    def own_copy(c, f):
        return remote(
            g_out.at[c, f], g_own.at[c, f], own_ssem.at[c, f], own_rsem.at[c, f], node, sec - 1)

    def par_copy(c, f):
        return remote(
            g_out.at[c, f], g_par.at[c, f], par_ssem.at[c, f], par_rsem.at[c, f], partner, sec - 1)

    def relay_copy(c, f):
        return remote(
            g_own.at[c, f], g_par.at[c, f], par_ssem.at[groups + c, f], par_rsem.at[c, f], partner)

    def line_copy(c, f):
        return remote(
            to_line.at[c, f], from_line.at[c, f], term_ssem.at[c, f], term_rsem.at[c, f], line_to)

    def build(c):
        @pl.when(odd)
        def _():
            for d, owner in enumerate((partner, outer)):
                for cb in range(blocks):
                    for r in range(blocks):
                        place = (d * blocks + cb) * blk
                        adj_out[c, place:place + blk, r * blk:(r + 1) * blk] = block(c, owner, cb, r)
            adj_copy(c).start()

        for cb in range(blocks):
            for r in range(blocks):
                adj_own[c, cb * blk:(cb + 1) * blk, r * blk:(r + 1) * blk] = block(c, node, cb, r)

    def take_top(c):
        for f in range(halves):
            g_own[c, f] = top_ref[c, :, f * width:(f + 1) * width]
            relay_copy(c, f).start()

    def forward(c):
        step = hidden // 4
        for j in range(4):
            at = slice(j * step, (j + 1) * step)
            pre = dot(acts_ref[0, c], w1_ref[0, :, at])
            sigma = jax.nn.sigmoid(pre)
            act_s[c, :, at] = (pre * sigma).astype(BF16)
            slope_s[c, :, at] = sigma * (1.0 + pre * (1.0 - sigma))

    def weight_grads(c):
        def put(ref, at, value):
            if c == 0:
                ref[at, :] = value
            else:
                ref[at, :] += value

        step = hidden // 4
        for j in range(4):
            at = slice(j * step, (j + 1) * step)
            put(acc2, at, dot(act_s[c, :, at], dm_s[c], CONTRACT_FIRST))
        step = feat // 4
        for j in range(4):
            at = slice(j * step, (j + 1) * step)
            put(acc1, at, dot(acts_ref[0, c, :, at], dpre_s[c], CONTRACT_FIRST))

    greeted = 4 + has_below.astype(jnp.int32) + below_top.astype(jnp.int32)
    pl.semaphore_wait(barrier, greeted)

    @pl.when(top_sec)
    def _():
        load(4, top_hbm, top_ref).wait()
        take_top(0)

    load_table.wait()
    build(0)
    load_acts.wait()
    load_w1.wait()
    load_w2.wait()

    @pl.when(below_top)
    def _():
        for c in range(1, groups):
            build(c)
        for c in range(groups):
            forward(c)

    for c in range(groups):
        @pl.when(below_top)
        def _():
            for f in range(halves):
                own_copy(c, f).wait_recv()
                pl.when(odd)(lambda: relay_copy(c, f).start())

        local = [dot(adj_own[c], g_own[c, f]) for f in range(halves)]
        adj_copy(c).wait_recv()
        pl.when(odd)(lambda: pass_copy(c).start())
        for f in range(halves):
            par_copy(c, f).wait_recv()
            to_line[c, f] = dot(adj_par[c, rows:], g_par[c, f]).astype(BF16)
            line_copy(c, f).start()
            local[f] = local[f] + dot(adj_par[c, :rows], g_par[c, f])

        @pl.when(top_sec)
        def _():
            if c + 1 < groups:
                take_top(c + 1)
                build(c + 1)
            forward(c)

        if c > 0:
            weight_grads(c - 1)
        for f in range(halves):
            line_copy(c, f).wait_recv()
            dm_s[c, :, f * width:(f + 1) * width] = (local[f] + from_line[c, f].astype(F32)).astype(BF16)
        step = hidden // 4
        for j in range(4):
            at = slice(j * step, (j + 1) * step)
            dact = dot(dm_s[c], w2_ref[0, at, :], CONTRACT_LAST)
            dpre_s[c, :, at] = (dact * slope_s[c, :, at]).astype(BF16)
        for f in range(halves):
            at = slice(f * width, (f + 1) * width)
            back = dot(dpre_s[c], w1_ref[0, at, :], CONTRACT_LAST)
            g_out[c, f] = (g_own[c, f].astype(F32) + back).astype(BF16)
            pl.when(has_below)(lambda: own_copy(c, f).start())
            pl.when(odd)(lambda: par_copy(c, f).start())
            grads_ref[0, c, :, at] = g_out[c, f]

    weight_grads(groups - 1)
    half1 = feat // 2
    half2 = hidden // 2
    step1 = half1 // CHUNKS
    step2 = half2 // CHUNKS

    def own(kind, j):
        if kind == 0:
            return pl.ds(pl.multiple_of(side * half1 + j * step1, step1), step1)
        return pl.ds(pl.multiple_of(side * half2 + j * step2, step2), step2)

    def other(kind, j):
        if kind == 0:
            return pl.ds(pl.multiple_of((1 - side) * half1 + j * step1, step1), step1)
        return pl.ds(pl.multiple_of((1 - side) * half2 + j * step2, step2), step2)

    acc = (acc1, acc2)
    outs = (first_ref, second_ref)
    send_x, recv_x = (send_x1, send_x2), (recv_x1, recv_x2)
    send_z, recv_z = (send_z1, send_z2), (recv_z1, recv_z2)
    towards = (node + 2, node - 2)
    away = (node - 2, node + 2)
    has_towards = (has_up, has_down)
    has_away = (has_down, has_up)

    def x_copy(kind, j):
        return remote(
            send_x[kind].at[j], recv_x[kind].at[j], x_ssem.at[kind, j], x_rsem.at[kind, j], partner)

    def z_copy(kind, j):
        return remote(
            send_z[kind].at[j], recv_z[kind].at[j], z_ssem.at[kind, j], z_rsem.at[kind, j], towards[kind])

    def az_copy(kind, j):
        place = outs[kind].at[own(kind, j), :]
        return remote(place, place, az_ssem.at[kind, j], az_rsem.at[kind, j], away[kind])

    def ax_copy(kind, j):
        place = outs[kind].at[own(kind, j), :]
        return remote(place, place, ax_ssem.at[kind, j], ax_rsem.at[kind, j], partner)

    def send_across(kind, j):
        send_x[kind][j] = acc[kind][other(kind, j), :].astype(BF16)
        x_copy(kind, j).start()

    def reduce_chunk(kind, j):
        value = acc[kind][own(kind, j), :] + recv_x[kind][j].astype(F32)
        send_z[kind][j] = value.astype(BF16)

        @pl.when(has_away[kind])
        def _():
            z_copy(kind, j).wait_recv()
            send_z[kind][j] = (value + recv_z[kind][j].astype(F32)).astype(BF16)

        @pl.when(has_towards[kind])
        def _():
            z_copy(kind, j).start()

        @pl.when(jnp.logical_not(has_towards[kind]))
        def _():
            outs[kind][own(kind, j), :] = send_z[kind][j]
            az_copy(kind, j).start()
            ax_copy(kind, j).start()

    def gather_chunk(kind, j):
        @pl.when(has_towards[kind])
        def _():
            az_copy(kind, j).wait_recv()
            pl.when(has_away[kind])(lambda: az_copy(kind, j).start())
            ax_copy(kind, j).start()

    def reduce_all(first):
        order = [(kind, j) for kind in (first, 1 - first) for j in range(CHUNKS)]
        for kind, j in order[:AHEAD]:
            send_across(kind, j)
        for i, (kind, j) in enumerate(order):
            x_copy(kind, j).wait_recv()
            if i + AHEAD < len(order):
                send_across(*order[i + AHEAD])
            reduce_chunk(kind, j)

    def gather_all(first):
        for kind in (first, 1 - first):
            for j in range(CHUNKS):
                gather_chunk(kind, j)

    early = along < line // 2
    late = jnp.logical_not(early)
    pl.when(early)(lambda: reduce_all(0))
    pl.when(late)(lambda: reduce_all(1))
    pl.when(early)(lambda: gather_all(1))
    pl.when(late)(lambda: gather_all(0))

    for kind in range(2):
        for j in range(CHUNKS):
            ax_copy(kind, j).wait()
            x_copy(kind, j).wait_send()
            pl.when(has_towards[kind])(lambda: z_copy(kind, j).wait_send())
            pl.when(has_away[kind])(lambda: az_copy(kind, j).wait_send())
    for c in range(groups):
        @pl.when(odd)
        def _():
            adj_copy(c).wait_send()
            pass_copy(c).wait_send()

        for f in range(halves):
            line_copy(c, f).wait_send()
            pl.when(has_below)(lambda: own_copy(c, f).wait_send())

            @pl.when(odd)
            def _():
                par_copy(c, f).wait_send()
                relay_copy(c, f).wait_send()


def shards(acts, top_grad, w_in, w_out, tile_table, tile_rows, tile_cols, tile_ids, tile_count):
    sections = lax.axis_size("section")
    nodes = lax.axis_size("node")
    groups, rows, feat = top_grad.shape
    hidden = w_in.shape[2]
    vmem = pl.BlockSpec(memory_space=pltpu.VMEM)
    hbm = pl.BlockSpec(memory_space=pltpu.HBM)
    smem = pl.BlockSpec(memory_space=pltpu.SMEM)
    width = feat // HALVES
    half = pltpu.VMEM((groups, HALVES, rows, width), BF16)
    wide = lambda kind, count: pltpu.VMEM((groups, rows, count), kind)
    part1 = pltpu.VMEM((CHUNKS, feat // 2 // CHUNKS, hidden), BF16)
    part2 = pltpu.VMEM((CHUNKS, hidden // 2 // CHUNKS, feat), BF16)
    dma = pltpu.SemaphoreType.DMA
    grads, first, second = pl.pallas_call(
        functools.partial(kernel, sections, nodes),
        out_shape=(
            jax.ShapeDtypeStruct((1, groups, rows, feat), BF16),
            jax.ShapeDtypeStruct((feat, hidden), BF16),
            jax.ShapeDtypeStruct((hidden, feat), BF16),
        ),
        in_specs=[smem] * 4 + [hbm] * 5,
        out_specs=(vmem, vmem, vmem),
        scratch_shapes=[
            *[pltpu.VMEM(arg.shape, BF16) for arg in (acts, top_grad, w_in, w_out, tile_table)],
            dma((5,)),
            pltpu.VMEM((groups, rows, rows), BF16),
            *[pltpu.VMEM((groups, 2 * rows, rows), BF16)] * 2,
            *[half] * 5,
            wide(BF16, hidden),
            wide(F32, hidden),
            wide(BF16, feat),
            wide(BF16, hidden),
            pltpu.VMEM((feat, hidden), F32),
            pltpu.VMEM((hidden, feat), F32),
            *[part1, part2] * 4,
            *[dma((groups,))] * 3,
            *[dma((groups, HALVES))] * 2,
            dma((2 * groups, HALVES)),
            *[dma((groups, HALVES))] * 3,
            *[dma((2, CHUNKS))] * 8,
        ],
        compiler_params=pltpu.CompilerParams(
            collective_id=0, has_side_effects=True, vmem_limit_bytes=62 * 1024 * 1024
        ),
        name="relay_back",
    )(tile_rows, tile_cols, tile_ids, tile_count, acts, top_grad, w_in, w_out, tile_table)
    return grads, first.astype(F32)[None], second.astype(F32)[None]


def solution(mesh):
    return jax.shard_map(
        shards,
        mesh=mesh,
        in_specs=(
            P("section", None, "node", None),
            P(None, "node", None),
            P("section", None, None),
            P("section", None, None),
            P(None, "node", None, None),
            P(None, "node"),
            P(None, "node"),
            P(None, "node"),
            P(None, "node"),
        ),
        out_specs=(
            P("section", None, "node", None),
            P("section", None, None),
            P("section", None, None),
        ),
        check_vma=False,
    )
```

```python
import functools

import jax
import jax.numpy as jnp
from jax import lax
from jax.experimental import pallas as pl
from jax.experimental.pallas import tpu as pltpu
from jax.sharding import PartitionSpec as P

MESH = pl.DeviceIdType.MESH
F32 = jnp.float32
BF16 = jnp.bfloat16
CHUNKS = 8
AHEAD = 6
HALVES = 2
CONTRACT_LAST = (((1,), (1,)), ((), ()))
CONTRACT_FIRST = (((0,), (0,)), ((), ()))


def dot(a, b, dims=(((1,), (0,)), ((), ()))):
    return lax.dot_general(a, b, dims, preferred_element_type=F32)


def kernel(
    sections, nodes,
    rows_ref, cols_ref, ids_ref, count_ref, acts_hbm, top_hbm, w1_hbm, w2_hbm, table_hbm,
    grads_ref, first_ref, second_ref,
    acts_ref, top_ref, w1_ref, w2_ref, table_ref, load_sem,
    adj_own, adj_out, adj_par, g_own, g_par, g_out, to_line, from_line, local_s, act_s, slope_s, dm_s, dpre_s, acc1, acc2,
    send_x1, send_x2, recv_x1, recv_x2, send_z1, send_z2, recv_z1, recv_z2,
    adj_ssem, adj_rsem, pass_ssem, own_ssem, own_rsem, par_ssem, par_rsem, term_ssem, term_rsem,
    x_ssem, x_rsem, z_ssem, z_rsem, az_ssem, az_rsem, ax_ssem, ax_rsem,
):
    groups, halves, rows, width = g_own.shape
    feat = halves * width
    hidden = w1_ref.shape[2]
    slots = rows_ref.shape[1]
    blk = table_ref.shape[-1]
    blocks = rows // blk
    sec = lax.axis_index("section")
    node = lax.axis_index("node")
    line = nodes // 2
    along = node // 2
    side = lax.rem(node, 2)
    partner = node + 1 - 2 * side
    outer = lax.rem(node + nodes - 1 + 2 * side, nodes)
    line_to = lax.rem(node + 2 + side * (nodes - 4), nodes)
    line_from = lax.rem(node + nodes - 2 + side * (4 - nodes) + side * nodes, nodes)
    top_sec = sec == sections - 1
    below_top = sec < sections - 1
    has_below = sec > 0
    odd = lax.rem(sec, 2) == 1
    even = lax.rem(sec, 2) == 0
    has_up = along < line - 1
    has_down = along > 0

    def remote(src, dst, ssem, rsem, node_to, sec_to=None):
        return pltpu.make_async_remote_copy(
            src_ref=src, dst_ref=dst, send_sem=ssem, recv_sem=rsem,
            device_id=(sec if sec_to is None else sec_to, node_to), device_id_type=MESH,
        )

    barrier = pltpu.get_barrier_semaphore()

    def greet(section_to, node_to):
        pl.semaphore_signal(barrier, inc=1, device_id=(section_to, node_to), device_id_type=MESH)

    greet(sec, partner)
    greet(sec, line_to)
    greet(sec, line_from)
    pl.when(odd)(lambda: greet(sec - 1, partner))
    pl.when(even)(lambda: greet(sec + 1, partner))
    pl.when(has_below)(lambda: greet(sec - 1, node))
    pl.when(below_top)(lambda: greet(sec + 1, node))

    def load(at, src, dst):
        return pltpu.make_async_copy(src, dst, load_sem.at[at])

    load_table = load(0, table_hbm, table_ref)
    load_acts = load(1, acts_hbm, acts_ref)
    load_w1 = load(2, w1_hbm, w1_ref)
    load_w2 = load(3, w2_hbm, w2_ref)
    load_table.start()
    pl.when(top_sec)(lambda: load(4, top_hbm, top_ref).start())
    load_acts.start()
    load_w1.start()
    load_w2.start()

    def block(c, owner, cb, r):
        total = jnp.zeros((blk, blk), F32)
        for k in range(slots):
            live = (k < count_ref[c, 0]) & (rows_ref[c, k] == r) & (cols_ref[c, k] == owner * blocks + cb)
            coef = jnp.where(live, 1.0, 0.0).astype(F32)
            total = total + coef * table_ref[c, ids_ref[c, k]].astype(F32)
        return total.T.astype(BF16)

    def adj_copy(c):
        return remote(adj_out.at[c], adj_par.at[c], adj_ssem.at[c], adj_rsem.at[c], partner)

    def pass_copy(c):
        return remote(adj_par.at[c], adj_par.at[c], pass_ssem.at[c], adj_rsem.at[c], node, sec - 1)

    def own_copy(c, f):
        return remote(
            g_out.at[c, f], g_own.at[c, f], own_ssem.at[c, f], own_rsem.at[c, f], node, sec - 1)

    def par_copy(c, f):
        return remote(
            g_out.at[c, f], g_par.at[c, f], par_ssem.at[c, f], par_rsem.at[c, f], partner, sec - 1)

    def relay_copy(c, f):
        return remote(
            g_own.at[c, f], g_par.at[c, f], par_ssem.at[groups + c, f], par_rsem.at[c, f], partner)

    def line_copy(c, f):
        return remote(
            to_line.at[c, f], from_line.at[c, f], term_ssem.at[c, f], term_rsem.at[c, f], line_to)

    def build(c):
        @pl.when(odd)
        def _():
            for d, owner in enumerate((partner, outer)):
                for cb in range(blocks):
                    for r in range(blocks):
                        place = (d * blocks + cb) * blk
                        adj_out[c, place:place + blk, r * blk:(r + 1) * blk] = block(c, owner, cb, r)
            adj_copy(c).start()

        for cb in range(blocks):
            for r in range(blocks):
                adj_own[c, cb * blk:(cb + 1) * blk, r * blk:(r + 1) * blk] = block(c, node, cb, r)

    def take_top(c):
        for f in range(halves):
            g_own[c, f] = top_ref[c, :, f * width:(f + 1) * width]
            relay_copy(c, f).start()

    def forward(c):
        step = hidden // 4
        for j in range(4):
            at = slice(j * step, (j + 1) * step)
            pre = dot(acts_ref[0, c], w1_ref[0, :, at])
            sigma = jax.nn.sigmoid(pre)
            act_s[c, :, at] = (pre * sigma).astype(BF16)
            slope_s[c, :, at] = sigma * (1.0 + pre * (1.0 - sigma))

    def weight_grads(c):
        def put(ref, at, value):
            if c == 0:
                ref[at, :] = value
            else:
                ref[at, :] += value

        step = hidden // 4
        for j in range(4):
            at = slice(j * step, (j + 1) * step)
            put(acc2, at, dot(act_s[c, :, at], dm_s[c], CONTRACT_FIRST))
        step = feat // 4
        for j in range(4):
            at = slice(j * step, (j + 1) * step)
            put(acc1, at, dot(acts_ref[0, c, :, at], dpre_s[c], CONTRACT_FIRST))

    greeted = 4 + has_below.astype(jnp.int32) + below_top.astype(jnp.int32)
    pl.semaphore_wait(barrier, greeted)

    def spread(c):
        @pl.when(below_top)
        def _():
            for f in range(halves):
                own_copy(c, f).wait_recv()
                pl.when(odd)(lambda: relay_copy(c, f).start())

        for f in range(halves):
            local_s[c, f] = dot(adj_own[c], g_own[c, f])
        adj_copy(c).wait_recv()
        pl.when(odd)(lambda: pass_copy(c).start())
        for f in range(halves):
            par_copy(c, f).wait_recv()
            to_line[c, f] = dot(adj_par[c, rows:], g_par[c, f]).astype(BF16)
            line_copy(c, f).start()
        for f in range(halves):
            local_s[c, f] += dot(adj_par[c, :rows], g_par[c, f])

    def mlp(c):
        for f in range(halves):
            line_copy(c, f).wait_recv()
            dm_s[c, :, f * width:(f + 1) * width] = (local_s[c, f] + from_line[c, f].astype(F32)).astype(BF16)
        step = hidden // 4
        for j in range(4):
            at = slice(j * step, (j + 1) * step)
            dact = dot(dm_s[c], w2_ref[0, at, :], CONTRACT_LAST)
            dpre_s[c, :, at] = (dact * slope_s[c, :, at]).astype(BF16)
        for f in range(halves):
            at = slice(f * width, (f + 1) * width)
            back = dot(dpre_s[c], w1_ref[0, at, :], CONTRACT_LAST)
            g_out[c, f] = (g_own[c, f].astype(F32) + back).astype(BF16)

            @pl.when(has_below)
            def _():
                own_copy(c, f).start()
                pl.when(odd)(lambda: par_copy(c, f).start())

            grads_ref[0, c, :, at] = g_out[c, f]

    @pl.when(top_sec)
    def _():
        load(4, top_hbm, top_ref).wait()
        take_top(0)

    load_table.wait()
    build(0)
    load_acts.wait()
    load_w1.wait()
    load_w2.wait()
    forward(0)

    @pl.when(below_top)
    def _():
        for c in range(1, groups):
            build(c)
        for c in range(1, groups):
            forward(c)

    def prepare(c):
        @pl.when(top_sec)
        def _():
            take_top(c)
            build(c)
            forward(c)

    if groups > 1:
        prepare(1)
    spread(0)
    for c in range(groups):
        if c + 2 < groups:
            prepare(c + 2)
        if c + 1 < groups:
            spread(c + 1)
        mlp(c)
        if c + 2 < groups:
            weight_grads(c)
    for c in range(max(groups - 2, 0), groups):
        weight_grads(c)

    half1 = feat // 2
    half2 = hidden // 2
    step1 = half1 // CHUNKS
    step2 = half2 // CHUNKS

    def own(kind, j):
        if kind == 0:
            return pl.ds(pl.multiple_of(side * half1 + j * step1, step1), step1)
        return pl.ds(pl.multiple_of(side * half2 + j * step2, step2), step2)

    def other(kind, j):
        if kind == 0:
            return pl.ds(pl.multiple_of((1 - side) * half1 + j * step1, step1), step1)
        return pl.ds(pl.multiple_of((1 - side) * half2 + j * step2, step2), step2)

    acc = (acc1, acc2)
    outs = (first_ref, second_ref)
    send_x, recv_x = (send_x1, send_x2), (recv_x1, recv_x2)
    send_z, recv_z = (send_z1, send_z2), (recv_z1, recv_z2)
    towards = (node + 2, node - 2)
    away = (node - 2, node + 2)
    has_towards = (has_up, has_down)
    has_away = (has_down, has_up)

    def x_copy(kind, j):
        return remote(
            send_x[kind].at[j], recv_x[kind].at[j], x_ssem.at[kind, j], x_rsem.at[kind, j], partner)

    def z_copy(kind, j):
        return remote(
            send_z[kind].at[j], recv_z[kind].at[j], z_ssem.at[kind, j], z_rsem.at[kind, j], towards[kind])

    def az_copy(kind, j):
        place = outs[kind].at[own(kind, j), :]
        return remote(place, place, az_ssem.at[kind, j], az_rsem.at[kind, j], away[kind])

    def ax_copy(kind, j):
        place = outs[kind].at[own(kind, j), :]
        return remote(place, place, ax_ssem.at[kind, j], ax_rsem.at[kind, j], partner)

    def send_across(kind, j):
        send_x[kind][j] = acc[kind][other(kind, j), :].astype(BF16)
        x_copy(kind, j).start()

    def reduce_chunk(kind, j):
        value = acc[kind][own(kind, j), :] + recv_x[kind][j].astype(F32)
        send_z[kind][j] = value.astype(BF16)

        @pl.when(has_away[kind])
        def _():
            z_copy(kind, j).wait_recv()
            send_z[kind][j] = (value + recv_z[kind][j].astype(F32)).astype(BF16)

        @pl.when(has_towards[kind])
        def _():
            z_copy(kind, j).start()

        @pl.when(jnp.logical_not(has_towards[kind]))
        def _():
            outs[kind][own(kind, j), :] = send_z[kind][j]
            az_copy(kind, j).start()
            ax_copy(kind, j).start()

    def gather_chunk(kind, j):
        @pl.when(has_towards[kind])
        def _():
            az_copy(kind, j).wait_recv()
            pl.when(has_away[kind])(lambda: az_copy(kind, j).start())
            ax_copy(kind, j).start()

    def reduce_all(first):
        order = [(kind, j) for kind in (first, 1 - first) for j in range(CHUNKS)]
        for kind, j in order[:AHEAD]:
            send_across(kind, j)
        for i, (kind, j) in enumerate(order):
            x_copy(kind, j).wait_recv()
            if i + AHEAD < len(order):
                send_across(*order[i + AHEAD])
            reduce_chunk(kind, j)

    def gather_all(first):
        for kind in (first, 1 - first):
            for j in range(CHUNKS):
                gather_chunk(kind, j)

    early = along < line // 2
    late = jnp.logical_not(early)
    pl.when(early)(lambda: reduce_all(0))
    pl.when(late)(lambda: reduce_all(1))
    pl.when(early)(lambda: gather_all(1))
    pl.when(late)(lambda: gather_all(0))

    for kind in range(2):
        for j in range(CHUNKS):
            ax_copy(kind, j).wait()
            x_copy(kind, j).wait_send()
            pl.when(has_towards[kind])(lambda: z_copy(kind, j).wait_send())
            pl.when(has_away[kind])(lambda: az_copy(kind, j).wait_send())
    for c in range(groups):
        @pl.when(odd)
        def _():
            adj_copy(c).wait_send()
            pass_copy(c).wait_send()

        for f in range(halves):
            line_copy(c, f).wait_send()
            pl.when(has_below)(lambda: own_copy(c, f).wait_send())

            @pl.when(odd)
            def _():
                par_copy(c, f).wait_send()
                relay_copy(c, f).wait_send()


def shards(acts, top_grad, w_in, w_out, tile_table, tile_rows, tile_cols, tile_ids, tile_count):
    sections = lax.axis_size("section")
    nodes = lax.axis_size("node")
    groups, rows, feat = top_grad.shape
    hidden = w_in.shape[2]
    vmem = pl.BlockSpec(memory_space=pltpu.VMEM)
    hbm = pl.BlockSpec(memory_space=pltpu.HBM)
    smem = pl.BlockSpec(memory_space=pltpu.SMEM)
    width = feat // HALVES
    half = pltpu.VMEM((groups, HALVES, rows, width), BF16)
    wide = lambda kind, count: pltpu.VMEM((groups, rows, count), kind)
    part1 = pltpu.VMEM((CHUNKS, feat // 2 // CHUNKS, hidden), BF16)
    part2 = pltpu.VMEM((CHUNKS, hidden // 2 // CHUNKS, feat), BF16)
    dma = pltpu.SemaphoreType.DMA
    grads, first, second = pl.pallas_call(
        functools.partial(kernel, sections, nodes),
        out_shape=(
            jax.ShapeDtypeStruct((1, groups, rows, feat), BF16),
            jax.ShapeDtypeStruct((feat, hidden), BF16),
            jax.ShapeDtypeStruct((hidden, feat), BF16),
        ),
        in_specs=[smem] * 4 + [hbm] * 5,
        out_specs=(vmem, vmem, vmem),
        scratch_shapes=[
            *[pltpu.VMEM(arg.shape, BF16) for arg in (acts, top_grad, w_in, w_out, tile_table)],
            dma((5,)),
            pltpu.VMEM((groups, rows, rows), BF16),
            *[pltpu.VMEM((groups, 2 * rows, rows), BF16)] * 2,
            *[half] * 5,
            pltpu.VMEM((groups, HALVES, rows, width), F32),
            wide(BF16, hidden),
            wide(F32, hidden),
            wide(BF16, feat),
            wide(BF16, hidden),
            pltpu.VMEM((feat, hidden), F32),
            pltpu.VMEM((hidden, feat), F32),
            *[part1, part2] * 4,
            *[dma((groups,))] * 3,
            *[dma((groups, HALVES))] * 2,
            dma((2 * groups, HALVES)),
            *[dma((groups, HALVES))] * 3,
            *[dma((2, CHUNKS))] * 8,
        ],
        compiler_params=pltpu.CompilerParams(
            collective_id=0, has_side_effects=True, vmem_limit_bytes=62 * 1024 * 1024
        ),
        name="relay_back",
    )(tile_rows, tile_cols, tile_ids, tile_count, acts, top_grad, w_in, w_out, tile_table)
    return grads, first.astype(F32)[None], second.astype(F32)[None]


def solution(mesh):
    return jax.shard_map(
        shards,
        mesh=mesh,
        in_specs=(
            P("section", None, "node", None),
            P(None, "node", None),
            P("section", None, None),
            P("section", None, None),
            P(None, "node", None, None),
            P(None, "node"),
            P(None, "node"),
            P(None, "node"),
            P(None, "node"),
        ),
        out_specs=(
            P("section", None, "node", None),
            P("section", None, None),
            P("section", None, None),
        ),
        check_vma=False,
    )
```

```python
import functools

import jax
import jax.numpy as jnp
from jax import lax
from jax.experimental import pallas as pl
from jax.experimental.pallas import tpu as pltpu
from jax.sharding import PartitionSpec as P

MESH = pl.DeviceIdType.MESH
F32 = jnp.float32
BF16 = jnp.bfloat16
PAIRED = 4
CHUNKS = 12
LAG = 3
HALVES = 2
CONTRACT_LAST = (((1,), (1,)), ((), ()))
CONTRACT_FIRST = (((0,), (0,)), ((), ()))


def dot(a, b, dims=(((1,), (0,)), ((), ()))):
    return lax.dot_general(a, b, dims, preferred_element_type=F32)


def kernel(
    sections, nodes,
    rows_ref, cols_ref, ids_ref, count_ref, acts_hbm, top_hbm, w1_hbm, w2_hbm, table_hbm,
    grads_ref, first_ref, second_ref,
    acts_ref, top_ref, w1_ref, w2_ref, table_ref, load_sem,
    adj_own, adj_out, adj_par, g_own, g_par, g_out, to_line, from_line, local_s, act_s, slope_s, dm_s, dpre_s, acc1, acc2,
    send_x1, send_x2, recv_x1, recv_x2, send_z1, send_z2, recv_z1, recv_z2,
    adj_ssem, adj_rsem, pass_ssem, own_ssem, own_rsem, par_ssem, par_rsem, term_ssem, term_rsem,
    x_ssem, x_rsem, z_ssem, z_rsem, az_ssem, az_rsem, ax_ssem, ax_rsem,
):
    groups, halves, rows, width = g_own.shape
    feat = halves * width
    hidden = w1_ref.shape[2]
    slots = rows_ref.shape[1]
    blk = table_ref.shape[-1]
    blocks = rows // blk
    sec = lax.axis_index("section")
    node = lax.axis_index("node")
    line = nodes // 2
    along = node // 2
    side = lax.rem(node, 2)
    partner = node + 1 - 2 * side
    outer = lax.rem(node + nodes - 1 + 2 * side, nodes)
    line_to = lax.rem(node + 2 + side * (nodes - 4), nodes)
    line_from = lax.rem(node + nodes - 2 + side * (4 - nodes) + side * nodes, nodes)
    top_sec = sec == sections - 1
    below_top = sec < sections - 1
    has_below = sec > 0
    odd = lax.rem(sec, 2) == 1
    even = lax.rem(sec, 2) == 0
    has_up = along < line - 1
    has_down = along > 0

    def remote(src, dst, ssem, rsem, node_to, sec_to=None):
        return pltpu.make_async_remote_copy(
            src_ref=src, dst_ref=dst, send_sem=ssem, recv_sem=rsem,
            device_id=(sec if sec_to is None else sec_to, node_to), device_id_type=MESH,
        )

    barrier = pltpu.get_barrier_semaphore()

    def greet(section_to, node_to):
        pl.semaphore_signal(barrier, inc=1, device_id=(section_to, node_to), device_id_type=MESH)

    greet(sec, partner)
    greet(sec, line_to)
    greet(sec, line_from)
    pl.when(odd)(lambda: greet(sec - 1, partner))
    pl.when(even)(lambda: greet(sec + 1, partner))
    pl.when(has_below)(lambda: greet(sec - 1, node))
    pl.when(below_top)(lambda: greet(sec + 1, node))

    def load(at, src, dst):
        return pltpu.make_async_copy(src, dst, load_sem.at[at])

    load_table = load(0, table_hbm, table_ref)
    load_acts = load(1, acts_hbm, acts_ref)
    load_w1 = load(2, w1_hbm, w1_ref)
    load_w2 = load(3, w2_hbm, w2_ref)
    load_table.start()
    pl.when(top_sec)(lambda: load(4, top_hbm, top_ref).start())
    load_acts.start()
    load_w1.start()
    load_w2.start()

    def block(c, owner, cb, r):
        total = jnp.zeros((blk, blk), F32)
        for k in range(slots):
            live = (k < count_ref[c, 0]) & (rows_ref[c, k] == r) & (cols_ref[c, k] == owner * blocks + cb)
            coef = jnp.where(live, 1.0, 0.0).astype(F32)
            total = total + coef * table_ref[c, ids_ref[c, k]].astype(F32)
        return total.T.astype(BF16)

    def adj_copy(c):
        return remote(adj_out.at[c], adj_par.at[c], adj_ssem.at[c], adj_rsem.at[c], partner)

    def pass_copy(c):
        return remote(adj_par.at[c], adj_par.at[c], pass_ssem.at[c], adj_rsem.at[c], node, sec - 1)

    def own_copy(c, f):
        return remote(
            g_out.at[c, f], g_own.at[c, f], own_ssem.at[c, f], own_rsem.at[c, f], node, sec - 1)

    def par_copy(c, f):
        return remote(
            g_out.at[c, f], g_par.at[c, f], par_ssem.at[c, f], par_rsem.at[c, f], partner, sec - 1)

    def relay_copy(c, f):
        return remote(
            g_own.at[c, f], g_par.at[c, f], par_ssem.at[groups + c, f], par_rsem.at[c, f], partner)

    def line_copy(c, f):
        return remote(
            to_line.at[c, f], from_line.at[c, f], term_ssem.at[c, f], term_rsem.at[c, f], line_to)

    def build(c):
        @pl.when(odd)
        def _():
            for d, owner in enumerate((partner, outer)):
                for cb in range(blocks):
                    for r in range(blocks):
                        place = (d * blocks + cb) * blk
                        adj_out[c, place:place + blk, r * blk:(r + 1) * blk] = block(c, owner, cb, r)
            adj_copy(c).start()

        for cb in range(blocks):
            for r in range(blocks):
                adj_own[c, cb * blk:(cb + 1) * blk, r * blk:(r + 1) * blk] = block(c, node, cb, r)

    def take_top(c):
        for f in range(halves):
            g_own[c, f] = top_ref[c, :, f * width:(f + 1) * width]
            relay_copy(c, f).start()

    def forward(c):
        step = hidden // 4
        for j in range(4):
            at = slice(j * step, (j + 1) * step)
            pre = dot(acts_ref[0, c], w1_ref[0, :, at])
            sigma = jax.nn.sigmoid(pre)
            act_s[c, :, at] = (pre * sigma).astype(BF16)
            slope_s[c, :, at] = sigma * (1.0 + pre * (1.0 - sigma))

    def weight_grads(c):
        def put(ref, at, value):
            if c == 0:
                ref[at, :] = value
            else:
                ref[at, :] += value

        step = hidden // 4
        for j in range(4):
            at = slice(j * step, (j + 1) * step)
            put(acc2, at, dot(act_s[c, :, at], dm_s[c], CONTRACT_FIRST))
        step = feat // 4
        for j in range(4):
            at = slice(j * step, (j + 1) * step)
            put(acc1, at, dot(acts_ref[0, c, :, at], dpre_s[c], CONTRACT_FIRST))

    greeted = 4 + has_below.astype(jnp.int32) + below_top.astype(jnp.int32)
    pl.semaphore_wait(barrier, greeted)

    def spread(c):
        @pl.when(below_top)
        def _():
            for f in range(halves):
                own_copy(c, f).wait_recv()
                pl.when(odd)(lambda: relay_copy(c, f).start())

        for f in range(halves):
            local_s[c, f] = dot(adj_own[c], g_own[c, f])
        adj_copy(c).wait_recv()
        pl.when(odd)(lambda: pass_copy(c).start())
        for f in range(halves):
            par_copy(c, f).wait_recv()
            to_line[c, f] = dot(adj_par[c, rows:], g_par[c, f]).astype(BF16)
            line_copy(c, f).start()
        for f in range(halves):
            local_s[c, f] += dot(adj_par[c, :rows], g_par[c, f])

    def mlp(c):
        for f in range(halves):
            line_copy(c, f).wait_recv()
            dm_s[c, :, f * width:(f + 1) * width] = (local_s[c, f] + from_line[c, f].astype(F32)).astype(BF16)
        step = hidden // 4
        for j in range(4):
            at = slice(j * step, (j + 1) * step)
            dact = dot(dm_s[c], w2_ref[0, at, :], CONTRACT_LAST)
            dpre_s[c, :, at] = (dact * slope_s[c, :, at]).astype(BF16)
        for f in range(halves):
            at = slice(f * width, (f + 1) * width)
            back = dot(dpre_s[c], w1_ref[0, at, :], CONTRACT_LAST)
            g_out[c, f] = (g_own[c, f].astype(F32) + back).astype(BF16)

            @pl.when(has_below)
            def _():
                own_copy(c, f).start()
                pl.when(odd)(lambda: par_copy(c, f).start())

            grads_ref[0, c, :, at] = g_out[c, f]

    @pl.when(top_sec)
    def _():
        load(4, top_hbm, top_ref).wait()
        take_top(0)

    load_table.wait()
    build(0)
    load_acts.wait()
    load_w1.wait()
    load_w2.wait()
    forward(0)

    @pl.when(below_top)
    def _():
        for c in range(1, groups):
            build(c)
        for c in range(1, groups):
            forward(c)

    def prepare(c):
        @pl.when(top_sec)
        def _():
            take_top(c)
            build(c)
            forward(c)

    if groups > 1:
        prepare(1)
    spread(0)
    for c in range(groups):
        if c + 2 < groups:
            prepare(c + 2)
        if c + 1 < groups:
            spread(c + 1)
        mlp(c)
        if c + 2 < groups:
            weight_grads(c)
    for c in range(max(groups - 2, 0), groups):
        weight_grads(c)

    step1, step2 = recv_x1.shape[1], recv_x2.shape[1]

    def place(kind, j, which):
        step = (step1, step2)[kind]
        if j < PAIRED:
            return pl.ds(pl.multiple_of((which * PAIRED + j) * step, step), step)
        return pl.ds((PAIRED + j) * step, step)

    def own(kind, j):
        return place(kind, j, side)

    def other(kind, j):
        return place(kind, j, 1 - side)

    acc = (acc1, acc2)
    outs = (first_ref, second_ref)
    send_x, recv_x = (send_x1, send_x2), (recv_x1, recv_x2)
    send_z, recv_z = (send_z1, send_z2), (recv_z1, recv_z2)
    towards = (node + 2, node - 2)
    away = (node - 2, node + 2)
    has_towards = (has_up, has_down)
    has_away = (has_down, has_up)

    def x_copy(kind, j):
        source = send_x if j < PAIRED else send_z
        return remote(
            source[kind].at[j], recv_x[kind].at[j], x_ssem.at[kind, j], x_rsem.at[kind, j], partner)

    def z_copy(kind, j):
        return remote(
            send_z[kind].at[j], recv_z[kind].at[j], z_ssem.at[kind, j], z_rsem.at[kind, j], towards[kind])

    def az_copy(kind, j):
        place = outs[kind].at[own(kind, j), :]
        return remote(place, place, az_ssem.at[kind, j], az_rsem.at[kind, j], away[kind])

    def ax_copy(kind, j):
        place = outs[kind].at[own(kind, j), :]
        return remote(place, place, ax_ssem.at[kind, j], ax_rsem.at[kind, j], partner)

    def send_across(kind, j):
        send_x[kind][j] = acc[kind][other(kind, j), :].astype(BF16)
        x_copy(kind, j).start()

    def reduce_chunk(kind, j):
        value = acc[kind][own(kind, j), :]
        if j < PAIRED:
            x_copy(kind, j).wait_recv()
            value = value + recv_x[kind][j].astype(F32)
        send_z[kind][j] = value.astype(BF16)

        @pl.when(has_away[kind])
        def _():
            z_copy(kind, j).wait_recv()
            send_z[kind][j] = (value + recv_z[kind][j].astype(F32)).astype(BF16)

        @pl.when(has_towards[kind])
        def _():
            z_copy(kind, j).start()

        @pl.when(jnp.logical_not(has_towards[kind]))
        def _():
            if j < PAIRED:
                outs[kind][own(kind, j), :] = send_z[kind][j]
                az_copy(kind, j).start()
                ax_copy(kind, j).start()
            else:
                x_copy(kind, j).start()

    def gather_chunk(kind, j):
        @pl.when(has_towards[kind])
        def _():
            az_copy(kind, j).wait_recv()
            pl.when(has_away[kind])(lambda: az_copy(kind, j).start())
            if j < PAIRED:
                ax_copy(kind, j).start()

    def finish_chunk(kind, j):
        @pl.when(jnp.logical_not(has_towards[kind]))
        def _():
            x_copy(kind, j).wait_recv()
            total = send_z[kind][j].astype(F32) + recv_x[kind][j].astype(F32)
            outs[kind][own(kind, j), :] = total.astype(BF16)
            az_copy(kind, j).start()

    chunks = [*range(PAIRED, CHUNKS), *range(PAIRED)]

    def reduce_all(first):
        order = [(kind, j) for kind in (first, 1 - first) for j in chunks]
        for kind, j in order:
            if j < PAIRED:
                send_across(kind, j)
        for i in range(len(order) + LAG):
            if i < len(order):
                reduce_chunk(*order[i])
            if i >= LAG and order[i - LAG][1] >= PAIRED:
                finish_chunk(*order[i - LAG])

    def gather_all(first):
        for kind in (first, 1 - first):
            for j in chunks:
                gather_chunk(kind, j)

    early = along < line // 2
    late = jnp.logical_not(early)
    pl.when(early)(lambda: reduce_all(0))
    pl.when(late)(lambda: reduce_all(1))
    pl.when(early)(lambda: gather_all(1))
    pl.when(late)(lambda: gather_all(0))

    for kind in range(2):
        for j in range(CHUNKS):
            if j < PAIRED:
                ax_copy(kind, j).wait()
                x_copy(kind, j).wait_send()
            else:
                pl.when(jnp.logical_not(has_towards[kind]))(lambda: x_copy(kind, j).wait_send())
            pl.when(has_towards[kind])(lambda: z_copy(kind, j).wait_send())
            pl.when(has_away[kind])(lambda: az_copy(kind, j).wait_send())
    for c in range(groups):
        @pl.when(odd)
        def _():
            adj_copy(c).wait_send()
            pass_copy(c).wait_send()

        for f in range(halves):
            line_copy(c, f).wait_send()
            pl.when(has_below)(lambda: own_copy(c, f).wait_send())

            @pl.when(odd)
            def _():
                par_copy(c, f).wait_send()
                relay_copy(c, f).wait_send()


def shards(acts, top_grad, w_in, w_out, tile_table, tile_rows, tile_cols, tile_ids, tile_count):
    sections = lax.axis_size("section")
    nodes = lax.axis_size("node")
    groups, rows, feat = top_grad.shape
    hidden = w_in.shape[2]
    vmem = pl.BlockSpec(memory_space=pltpu.VMEM)
    hbm = pl.BlockSpec(memory_space=pltpu.HBM)
    smem = pl.BlockSpec(memory_space=pltpu.SMEM)
    width = feat // HALVES
    half = pltpu.VMEM((groups, HALVES, rows, width), BF16)
    wide = lambda kind, count: pltpu.VMEM((groups, rows, count), kind)
    part1 = pltpu.VMEM((CHUNKS, feat // (CHUNKS + PAIRED), hidden), BF16)
    part2 = pltpu.VMEM((CHUNKS, hidden // (CHUNKS + PAIRED), feat), BF16)
    dma = pltpu.SemaphoreType.DMA
    grads, first, second = pl.pallas_call(
        functools.partial(kernel, sections, nodes),
        out_shape=(
            jax.ShapeDtypeStruct((1, groups, rows, feat), BF16),
            jax.ShapeDtypeStruct((feat, hidden), BF16),
            jax.ShapeDtypeStruct((hidden, feat), BF16),
        ),
        in_specs=[smem] * 4 + [hbm] * 5,
        out_specs=(vmem, vmem, vmem),
        scratch_shapes=[
            *[pltpu.VMEM(arg.shape, BF16) for arg in (acts, top_grad, w_in, w_out, tile_table)],
            dma((5,)),
            pltpu.VMEM((groups, rows, rows), BF16),
            *[pltpu.VMEM((groups, 2 * rows, rows), BF16)] * 2,
            *[half] * 5,
            pltpu.VMEM((groups, HALVES, rows, width), F32),
            wide(BF16, hidden),
            wide(F32, hidden),
            wide(BF16, feat),
            wide(BF16, hidden),
            pltpu.VMEM((feat, hidden), F32),
            pltpu.VMEM((hidden, feat), F32),
            *[part1, part2] * 4,
            *[dma((groups,))] * 3,
            *[dma((groups, HALVES))] * 2,
            dma((2 * groups, HALVES)),
            *[dma((groups, HALVES))] * 3,
            *[dma((2, CHUNKS))] * 8,
        ],
        compiler_params=pltpu.CompilerParams(
            collective_id=0, has_side_effects=True, vmem_limit_bytes=62 * 1024 * 1024
        ),
        name="relay_back",
    )(tile_rows, tile_cols, tile_ids, tile_count, acts, top_grad, w_in, w_out, tile_table)
    return grads, first.astype(F32)[None], second.astype(F32)[None]


def solution(mesh):
    return jax.shard_map(
        shards,
        mesh=mesh,
        in_specs=(
            P("section", None, "node", None),
            P(None, "node", None),
            P("section", None, None),
            P("section", None, None),
            P(None, "node", None, None),
            P(None, "node"),
            P(None, "node"),
            P(None, "node"),
            P(None, "node"),
        ),
        out_specs=(
            P("section", None, "node", None),
            P("section", None, None),
            P("section", None, None),
        ),
        check_vma=False,
    )
```
